32 devices in a mesh: sub: 16 (over z, y, core), rng: 2 (over x).
Axes of the slice: x: 2, y: 2, z: 4, core: 2. Of those that a mesh axis runs over, the one named last changes fastest.
Arguments:
- polar_image: float32 [2, 16, 256, 2048], P(None, 'sub', None, 'rng'), may hold values from -6 to 6
- beam_tap: int32 [3, 2, 512], replicated, may hold values from 0 to 254, as said below
- beam_frac: float32 [3, 2, 512], replicated, may hold values from 0 to 1
- range_shift: int32 [3, 2, 512], replicated, may hold values from -24 to 24
- range_weight: float32 [3, 2, 4, 512], replicated, may hold values from 0.05 to 0.45
- phase_rate: float32 [3, 2, 512], replicated, may hold values from -16 to 16
- phase_offset: float32 [3, 2, 512], replicated, may hold values from -0.5 to 0.5
Outputs:
- merged: float32 [2, 16, 256, 2048], P(None, 'sub', None, 'rng')
The draws below stay inside these ranges and needn't reach their ends.
Inputs may be any that keep to these rules, and one draw needn't show every extreme that they name: For output position p, beam_tap and beam_tap + 1 lie in the aligned group of child beams 4 (p // 8) to 4 (p // 8) + 3.
All inputs are finite; a program needn't handle non-finite values.
Results may differ from the reference program's by a relative error of at most 0.0003.
Values sent between devices are 32-bit elements; how exact they have to be, the bound alone decides.
A program may use at most 64 MiB of HBM per device.

```python
import math
import jax
import jax.numpy as jnp
from jax import lax

BEAMS = 256
RANGE = 2048
SECTIONS = 3
SHIFT = 24
SUBAPS = 16


def draw_beam_tap(key, part):
    slots = jnp.arange(2 * BEAMS, dtype=jnp.int32)
    jitter = jax.random.randint(key, (SECTIONS, 2, 2 * BEAMS), 0, 3, dtype=jnp.int32)
    jitter = jitter.at[:, :, 0].set(0).at[:, :, -1].set(2)
    return slots // 8 * 4 + jitter


def draw_range_shift(key, part):
    values = jax.random.randint(key, (SECTIONS, 2, 2 * BEAMS), -SHIFT, SHIFT + 1, dtype=jnp.int32)
    return values.at[:, :, 0].set(-SHIFT).at[:, :, -1].set(SHIFT)


def steps_of(key, dims, shards, smallest, high):
    level, own = 1.0, jax.random.fold_in(key, 6)
    for dim, parts in shards:
        steps = jnp.exp(jax.random.uniform(jax.random.fold_in(own, dim), (parts,), jnp.float32, smallest / len(shards), high / len(shards)))
        level = level * jnp.repeat(steps, dims[dim] // parts).reshape([-1 if axis == dim else 1 for axis in range(len(dims))])
    return level


def normal_values(key, dims, width, most, split=(), kind=jnp.bfloat16):
    entries = width * jax.random.normal(key, dims, jnp.float32)
    if split:
        entries = entries * steps_of(key, dims, split, -0.22, 0.18)
    return jnp.clip(entries, -most, most).astype(kind)


def setup_inputs(seed: int = 0) -> dict:
    key_list = jax.random.split(jax.random.key(seed), 8)
    return {
        "polar_image": normal_values(key_list[0], (2, SUBAPS, BEAMS, RANGE), 1.0, 6.0, ((1, 16), (3, 2)), jnp.float32),
        "beam_tap": draw_beam_tap(jax.random.fold_in(key_list[7], 71), 0),
        "beam_frac": jnp.clip(jax.random.uniform(key_list[2], (SECTIONS, 2, 2 * BEAMS), jnp.float32, 0.0, 1.0), 0.0, 1.0),
        "range_shift": draw_range_shift(jax.random.fold_in(key_list[7], 71), 0),
        "range_weight": jnp.clip(jax.random.uniform(key_list[4], (SECTIONS, 2, 4, 2 * BEAMS), jnp.float32, 0.05, 0.45), 0.05, 0.45),
        "phase_rate": jnp.clip(jax.random.uniform(key_list[5], (SECTIONS, 2, 2 * BEAMS), jnp.float32, -16.0, 16.0), -16.0, 16.0),
        "phase_offset": jnp.clip(jax.random.uniform(key_list[6], (SECTIONS, 2, 2 * BEAMS), jnp.float32, -0.5, 0.5), -0.5, 0.5),
    }


def contribution(child_data, beam_taps, fraction, shifts, weights, rates, offsets, col_start, count, margin):
    in_beams = child_data.shape[-2]
    beam_ids = jnp.arange(in_beams, dtype=jnp.int32)[None, :]
    lower_hit = (beam_ids == beam_taps[:, None]).astype(jnp.float32)
    upper_hit = (beam_ids == (beam_taps + 1)[:, None]).astype(jnp.float32)
    interp = (1.0 - fraction)[:, None] * lower_hit + fraction[:, None] * upper_hit
    angled = jnp.matmul(interp, child_data, precision=lax.Precision.HIGHEST)
    nbits = max((2 * SHIFT).bit_length(), 1)
    reach = 2 ** nbits - 1
    base = margin - SHIFT - 1
    moved = angled[..., base:]
    extra = count + 3 + reach - moved.shape[-1]
    if extra > 0:
        pad_spec = [(0, 0)] * (moved.ndim - 1) + [(0, extra)]
        moved = jnp.pad(moved, pad_spec)
    offset_rows = (shifts + SHIFT).astype(jnp.int32)
    length = count + 3 + reach
    moved = moved[..., :length]
    for bit_no in range(nbits):
        step = 2 ** bit_no
        length = length - step
        flag = (((offset_rows >> bit_no) & 1) == 1)[:, None]
        moved = jnp.where(flag, moved[..., step:step + length], moved[..., :length])
    ranged = None
    for tap_no in range(4):
        weighted = weights[tap_no][:, None] * moved[..., tap_no:tap_no + count]
        ranged = weighted if ranged is None else ranged + weighted
    position = ((col_start + jnp.arange(count, dtype=jnp.int32)).astype(jnp.float32) + 0.5) / RANGE
    angle_rad = (2.0 * math.pi) * (rates[:, None] * position[None, :] + offsets[:, None])
    cosine = jnp.cos(angle_rad)
    sine_part = jnp.sin(angle_rad)
    real_part = ranged[0] * cosine - ranged[1] * sine_part
    imag_part = ranged[0] * sine_part + ranged[1] * cosine
    return jnp.stack((real_part, imag_part))


def reference(polar_image, beam_tap, beam_frac, range_shift, range_weight, phase_rate, phase_offset):
    margin = SHIFT + 2
    current = polar_image
    for section_no in range(SECTIONS):
        blocks = 2 ** section_no
        half_rows = SUBAPS // (2 * blocks)
        grouped = current.reshape(2, blocks, 2, half_rows, BEAMS, RANGE)
        pair_stack = jnp.transpose(grouped, (1, 3, 2, 0, 4, 5)).reshape(blocks * half_rows, 2, 2, BEAMS, RANGE)

        def merge_pair(pair_data, section_no=section_no):
            summed = None
            for child_no in range(2):
                padded = jnp.pad(pair_data[child_no], ((0, 0), (0, 0), (margin, margin)))
                weighted = contribution(padded, beam_tap[section_no, child_no], beam_frac[section_no, child_no],
                                        range_shift[section_no, child_no], range_weight[section_no, child_no],
                                        phase_rate[section_no, child_no], phase_offset[section_no, child_no],
                                        0, RANGE, margin)
                summed = weighted if summed is None else summed + weighted
            return summed.reshape(2, 2, BEAMS, RANGE)

        outputs = lax.map(merge_pair, pair_stack)
        outputs = outputs.reshape(blocks, half_rows, 2, 2, BEAMS, RANGE)
        current = jnp.transpose(outputs, (2, 0, 3, 1, 4, 5)).reshape(2, SUBAPS, BEAMS, RANGE)
    return current
```

```python
import functools
import math

import jax
import jax.numpy as jnp
from jax import lax
from jax.experimental import pallas as pl
from jax.experimental.pallas import tpu as pltpu
from jax.sharding import PartitionSpec as P

SECTIONS = 3
SHIFT = 24
WAYS = 2**SECTIONS
TAPS = 4
LANES = 128
MOVES = (43, 43, 42)
FIELDS = 16
MESH = pl.DeviceIdType.MESH
WEIGHT, BLEND, FIRST, COS, SIN, STEP_COS, STEP_SIN, PLANES = 0, 4, 8, 9, 10, 11, 12, 13


def flipped(place, mask):
    for bit in range(SECTIONS):
        if mask >> bit & 1:
            place = place + (1 << bit) * (1 - 2 * (place // (1 << bit) % 2))
    return place


def cos_sin(cycles):
    half = (cycles - jnp.round(cycles)) * math.pi
    sq = half * half
    s = jnp.full_like(half, -1.0 / math.factorial(11))
    for n in (9, 7, 5, 3, 1):
        s = s * sq + (1.0 if n % 4 == 1 else -1.0) / math.factorial(n)
    s = s * half
    c = jnp.full_like(half, 1.0 / math.factorial(12))
    for n in (10, 8, 6, 4, 2, 0):
        c = c * sq + (1.0 if n % 4 == 0 else -1.0) / math.factorial(n)
    return 1.0 - 2.0 * s * s, 2.0 * s * c


def lane_take(x, idx):
    return jnp.take_along_axis(x, idx, axis=1, mode="promise_in_bounds")


def kernel(
    group_step, chunk, span,
    img, tap, frac, shift, wgt, rate, off, out,
    x0, x1, x2, x3, tmp, tab, coef,
    send_sem, recv_sem, own_sem, halo_send, halo_recv, out_sem,
):
    me, col = lax.axis_index("sub"), lax.axis_index("rng")
    place, inner = me // group_step, me % group_step
    row_len = img.shape[3]
    eighth = x0.shape[2]
    chunks = eighth // chunk
    width = x0.shape[3]
    blocks = width // LANES
    other = 1 - col
    col_base = col * (row_len - LANES)
    own_at = pl.multiple_of(col * LANES, LANES)

    def sub_of(p):
        return p * group_step + inner

    barrier = pltpu.get_barrier_semaphore()
    for x in range(1, WAYS):
        pl.semaphore_signal(barrier, inc=1, device_id=(sub_of(flipped(place, x)), col), device_id_type=MESH)
    pl.semaphore_signal(barrier, inc=1, device_id=(me, other), device_id_type=MESH)

    def own_copy(c):
        return pltpu.make_async_copy(
            img.at[:, 0, pl.ds(pl.multiple_of(place * eighth + c * chunk, 8), chunk), :],
            x0.at[:, place, pl.ds(c * chunk, chunk), pl.ds(own_at, row_len)],
            own_sem.at[c],
        )

    def piece(c, x, sending):
        peer = flipped(place, x)
        row = place if sending else peer
        return pltpu.make_async_remote_copy(
            src_ref=img.at[:, 0, pl.ds(pl.multiple_of(peer * eighth + c * chunk, 8), chunk), :],
            dst_ref=x0.at[:, row, pl.ds(c * chunk, chunk), pl.ds(own_at, row_len)],
            send_sem=send_sem.at[c, x],
            recv_sem=recv_sem.at[c, x],
            device_id=(sub_of(peer), col),
            device_id_type=MESH,
        )

    def halo(c, sending):
        src = pl.multiple_of((1 - col) * (row_len - LANES) + col * LANES, LANES)
        who = col if sending else other
        dst = pl.multiple_of(who * row_len, LANES)
        return pltpu.make_async_remote_copy(
            src_ref=x0.at[:, :, pl.ds(c * chunk, chunk), pl.ds(src, LANES)],
            dst_ref=x0.at[:, :, pl.ds(c * chunk, chunk), pl.ds(dst, LANES)],
            send_sem=halo_send.at[c],
            recv_sem=halo_recv.at[c],
            device_id=(me, other),
            device_id_type=MESH,
        )

    for c in range(chunks):
        own_copy(c).start()
    pl.semaphore_wait(barrier, WAYS)
    order = (4, 5, 6, 7, 2, 3, 1)
    for c in range(chunks):
        for x in order:
            piece(c, x, True).start()

    tmp[...] = jnp.zeros_like(tmp)
    for k in range(SECTIONS):
        for j in range(2):
            base = (k * 2 + j) * FIELDS
            tmp[base : base + 1, :] = tap[k, j : j + 1, :].astype(jnp.float32)
            tmp[base + 1 : base + 2, :] = frac[k, j : j + 1, :]
            tmp[base + 2 : base + 3, :] = shift[k, j : j + 1, :].astype(jnp.float32)
            tmp[base + 3 : base + 7, :] = wgt[k, j]
            tmp[base + 7 : base + 8, :] = rate[k, j : j + 1, :]
            tmp[base + 8 : base + 9, :] = off[k, j : j + 1, :]
    for n in range(tab.shape[0] // LANES):
        tab[n * LANES : (n + 1) * LANES, :] = tmp[:, n * LANES : (n + 1) * LANES].T
    lane = lax.broadcasted_iota(jnp.int32, (8, LANES), 1)

    at = []
    first_group = 0
    moved = LANES
    for k in range(SECTIONS):
        in_beams = eighth << k
        remaining = place % (1 << (SECTIONS - k))
        in_start = remaining * in_beams
        groups = in_beams // 4
        moved -= MOVES[k]
        at.append((first_group, groups, moved))

        def plan(g, carry, k=k, in_start=in_start, groups=groups, first=first_group, moved=moved):
            rows = tab[pl.ds(pl.multiple_of(2 * in_start + 8 * g, 8), 8), :]
            for j in range(2):
                def field(q):
                    n = (k * 2 + j) * FIELDS + q
                    return jnp.broadcast_to(rows[:, n : n + 1], (8, LANES))
                to = first + j * groups + g
                local = field(0) - (in_start + 4 * g).astype(jnp.float32)
                f = field(1)
                for b in range(4):
                    coef[to, BLEND + b] = jnp.where(local == b, 1.0 - f, 0.0) + jnp.where(local == b - 1, f, 0.0)
                coef[to, FIRST] = field(2) + float(SHIFT + MOVES[k] - SHIFT - 1)
                for t in range(TAPS):
                    coef[to, WEIGHT + t] = field(3 + t)
                r = (lane - moved + col_base).astype(jnp.float32) + 0.5
                cyc = field(7)
                c0, s0 = cos_sin(cyc * (r / span) + field(8))
                c1, s1 = cos_sin(cyc * (LANES / span))
                coef[to, COS] = c0
                coef[to, SIN] = s0
                coef[to, STEP_COS] = c1
                coef[to, STEP_SIN] = s1
            return carry

        lax.fori_loop(0, groups, plan, 0)
        first_group += 2 * groups

    def merge(k, src, dst, row, rows, g, half):
        first, groups, left = at[k]
        count = blocks + 1 if k < SECTIONS - 1 else blocks
        grp = 2 * g + half
        for j in range(2):
            to = first + j * groups + grp
            d0 = coef[to, FIRST].astype(jnp.int32)
            idx = [(lane + (d0 + t)) & (LANES - 1) for t in range(TAPS)]
            nxt = [lane < d0 + t for t in range(TAPS)]
            w = [coef[to, WEIGHT + t] for t in range(TAPS)]
            bl = [coef[to, BLEND + b] for b in range(4)]
            pc, ps = coef[to, COS], coef[to, SIN]
            sc, ss = coef[to, STEP_COS], coef[to, STEP_SIN]

            def angled(ch, block):
                block = block - 1 if k == 0 else block
                if block < 0 or (block + 1) * LANES > src.shape[3]:
                    return jnp.zeros((8, LANES), jnp.float32)
                tile = src[ch, rows[j], pl.ds(pl.multiple_of(8 * g, 8), 8), block * LANES : (block + 1) * LANES]
                total = None
                for b in range(4):
                    term = bl[b] * jnp.broadcast_to(tile[4 * half + b : 4 * half + b + 1, :], (8, LANES))
                    total = term if total is None else total + term
                return total

            cur = [angled(ch, 0) for ch in range(2)]
            for block in range(count):
                ahead = [angled(ch, block + 1) for ch in range(2)]
                ranged = []
                for ch in range(2):
                    total = None
                    for t in range(TAPS):
                        term = w[t] * lane_take(jnp.where(nxt[t], ahead[ch], cur[ch]), idx[t])
                        total = term if total is None else total + term
                    ranged.append(total)
                re = ranged[0] * pc - ranged[1] * ps
                im = ranged[0] * ps + ranged[1] * pc
                place_at = (pl.ds(pl.multiple_of(8 * grp, 8), 8), slice(block * LANES, (block + 1) * LANES))
                if j == 1:
                    re = re + dst[0, row, place_at[0], place_at[1]]
                    im = im + dst[1, row, place_at[0], place_at[1]]
                    if k < SECTIONS - 1 and block in (0, count - 1):
                        r = lane + (block * LANES - left + col_base)
                        inside = (r >= 0) & (r < span)
                        re = jnp.where(inside, re, 0.0)
                        im = jnp.where(inside, im, 0.0)
                dst[0, row, place_at[0], place_at[1]] = re
                dst[1, row, place_at[0], place_at[1]] = im
                if block < count - 1:
                    pc, ps = pc * sc - ps * ss, pc * ss + ps * sc
                cur = ahead

    def out_copy(c):
        n = chunk * WAYS
        return pltpu.make_async_copy(
            x3.at[:, 0, pl.ds(c * n, n), pl.ds(own_at, row_len)],
            out.at[:, 0, pl.ds(c * n, n), :],
            out_sem.at[c],
        )

    def compute(c):
        buffers = (x0, x1, x2, x3)
        for k in range(SECTIONS):
            n_rows = WAYS >> (k + 1)
            pairs = (chunk << k) // 8

            def body(it, carry, k=k, n_rows=n_rows, pairs=pairs):
                row, g = it // pairs, it % pairs
                for half in range(2):
                    merge(k, buffers[k], buffers[k + 1], row, (row, row + n_rows), c * pairs + g, half)
                return carry

            lax.fori_loop(0, n_rows * pairs, body, 0)
        out_copy(c).start()

    def arrive(c):
        own_copy(c).wait()
        for x in order:
            piece(c, x, False).wait_recv()
        halo(c, True).start()

    arrive(0)
    for c in range(chunks):
        if c + 1 < chunks:
            halo(c, False).wait_recv()
            compute(c)
            arrive(c + 1)
        else:
            halo(c, False).wait_recv()
            compute(c)
    for c in range(chunks):
        for x in order:
            piece(c, x, True).wait_send()
        halo(c, True).wait_send()
        out_copy(c).wait()


def on_device(polar_image, beam_tap, beam_frac, range_shift, range_weight, phase_rate, phase_offset):
    _, sub_count, beams, row_len = polar_image.shape
    eighth = beams // WAYS
    chunk = 8
    chunks = eighth // chunk
    group_step = lax.axis_size("sub") // WAYS
    width = row_len + LANES
    positions = beam_tap.shape[2]
    vmem = pl.BlockSpec(memory_space=pltpu.VMEM)
    hbm = pl.BlockSpec(memory_space=pl.ANY)
    n_groups = sum(2 * ((eighth << k) // 4) for k in range(SECTIONS))
    return pl.pallas_call(
        functools.partial(kernel, group_step, chunk, row_len * lax.axis_size("rng")),
        out_shape=jax.ShapeDtypeStruct(polar_image.shape, jnp.float32),
        in_specs=[hbm] + [vmem] * 6,
        out_specs=hbm,
        scratch_shapes=[
            pltpu.VMEM((2, WAYS, eighth, width), jnp.float32),
            pltpu.VMEM((2, WAYS // 2, 2 * eighth, width + LANES), jnp.float32),
            pltpu.VMEM((2, WAYS // 4, 4 * eighth, width + LANES), jnp.float32),
            pltpu.VMEM((2, 1, beams, width), jnp.float32),
            pltpu.VMEM((LANES, positions), jnp.float32),
            pltpu.VMEM((positions, LANES), jnp.float32),
            pltpu.VMEM((n_groups, PLANES, 8, LANES), jnp.float32),
            pltpu.SemaphoreType.DMA((chunks, WAYS)),
            pltpu.SemaphoreType.DMA((chunks, WAYS)),
            pltpu.SemaphoreType.DMA((chunks,)),
            pltpu.SemaphoreType.DMA((chunks,)),
            pltpu.SemaphoreType.DMA((chunks,)),
            pltpu.SemaphoreType.DMA((chunks,)),
        ],
        compiler_params=pltpu.CompilerParams(
            collective_id=0, has_side_effects=True, vmem_limit_bytes=48 * 2**20
        ),
    )(polar_image, beam_tap, beam_frac, range_shift, range_weight, phase_rate, phase_offset)


def solution(mesh):
    placed = (P(None, "sub", None, "rng"), P(), P(), P(), P(), P(), P())
    return jax.shard_map(
        on_device,
        mesh=mesh,
        in_specs=placed,
        out_specs=P(None, "sub", None, "rng"),
        check_vma=False,
    )
```

```python
import functools
import math

import jax
import jax.numpy as jnp
from jax import lax
from jax.experimental import pallas as pl
from jax.experimental.pallas import tpu as pltpu
from jax.sharding import PartitionSpec as P

SECTIONS = 3
SHIFT = 24
WAYS = 2**SECTIONS
TAPS = 4
LANES = 128
MOVES = (43, 43, 42)
FIELDS = 16
MESH = pl.DeviceIdType.MESH
WEIGHT, BLEND, FIRST, COS, SIN, STEP_COS, STEP_SIN, PLANES = 0, 4, 8, 9, 10, 11, 12, 13


def flipped(place, mask):
    for bit in range(SECTIONS):
        if mask >> bit & 1:
            place = place + (1 << bit) * (1 - 2 * (place // (1 << bit) % 2))
    return place


def cos_sin(cycles):
    half = (cycles - jnp.round(cycles)) * math.pi
    sq = half * half
    s = jnp.full_like(half, -1.0 / math.factorial(11))
    for n in (9, 7, 5, 3, 1):
        s = s * sq + (1.0 if n % 4 == 1 else -1.0) / math.factorial(n)
    s = s * half
    c = jnp.full_like(half, 1.0 / math.factorial(12))
    for n in (10, 8, 6, 4, 2, 0):
        c = c * sq + (1.0 if n % 4 == 0 else -1.0) / math.factorial(n)
    return 1.0 - 2.0 * s * s, 2.0 * s * c


def lane_take(x, idx):
    return jnp.take_along_axis(x, idx, axis=1, mode="promise_in_bounds")


def kernel(
    group_step, chunk, span,
    img, tap_in, frac_in, shift_in, wgt_in, rate_in, off_in, out,
    tap, frac, shift, wgt, rate, off,
    x0, x1, x2, x3, tmp, tab, coef,
    table_sem, send_sem, recv_sem, own_sem, halo_send, halo_recv, out_sem,
):
    me, col = lax.axis_index("sub"), lax.axis_index("rng")
    place, inner = me // group_step, me % group_step
    row_len = img.shape[3]
    eighth = x0.shape[2]
    chunks = eighth // chunk
    width = x0.shape[3]
    blocks = width // LANES
    other = 1 - col
    col_base = col * (row_len - LANES)
    own_at = pl.multiple_of(col * LANES, LANES)

    def sub_of(p):
        return p * group_step + inner

    barrier = pltpu.get_barrier_semaphore()
    for x in range(1, WAYS):
        pl.semaphore_signal(barrier, inc=1, device_id=(sub_of(flipped(place, x)), col), device_id_type=MESH)
    pl.semaphore_signal(barrier, inc=1, device_id=(me, other), device_id_type=MESH)

    def own_copy(c):
        return pltpu.make_async_copy(
            img.at[:, 0, pl.ds(pl.multiple_of(place * eighth + c * chunk, 8), chunk), :],
            x0.at[:, place, pl.ds(c * chunk, chunk), pl.ds(own_at, row_len)],
            own_sem.at[c],
        )

    def piece(c, x, sending):
        peer = flipped(place, x)
        row = place if sending else peer
        return pltpu.make_async_remote_copy(
            src_ref=img.at[:, 0, pl.ds(pl.multiple_of(peer * eighth + c * chunk, 8), chunk), :],
            dst_ref=x0.at[:, row, pl.ds(c * chunk, chunk), pl.ds(own_at, row_len)],
            send_sem=send_sem.at[c, x],
            recv_sem=recv_sem.at[c, x],
            device_id=(sub_of(peer), col),
            device_id_type=MESH,
        )

    def halo(c, sending):
        src = pl.multiple_of((1 - col) * (row_len - LANES) + col * LANES, LANES)
        who = col if sending else other
        dst = pl.multiple_of(who * row_len, LANES)
        return pltpu.make_async_remote_copy(
            src_ref=x0.at[:, :, pl.ds(c * chunk, chunk), pl.ds(src, LANES)],
            dst_ref=x0.at[:, :, pl.ds(c * chunk, chunk), pl.ds(dst, LANES)],
            send_sem=halo_send.at[c],
            recv_sem=halo_recv.at[c],
            device_id=(me, other),
            device_id_type=MESH,
        )

    tables = [
        pltpu.make_async_copy(a, b, table_sem.at[n])
        for n, (a, b) in enumerate(
            zip((tap_in, frac_in, shift_in, wgt_in, rate_in, off_in), (tap, frac, shift, wgt, rate, off))
        )
    ]
    for copy in tables:
        copy.start()
    pl.semaphore_wait(barrier, WAYS)
    order = (4, 5, 6, 7, 2, 3, 1)
    for c in range(chunks):
        for x in order:
            piece(c, x, True).start()
        own_copy(c).start()
    for copy in tables:
        copy.wait()

    tmp[...] = jnp.zeros_like(tmp)
    for k in range(SECTIONS):
        for j in range(2):
            base = (k * 2 + j) * FIELDS
            tmp[base : base + 1, :] = tap[k, j : j + 1, :].astype(jnp.float32)
            tmp[base + 1 : base + 2, :] = frac[k, j : j + 1, :]
            tmp[base + 2 : base + 3, :] = shift[k, j : j + 1, :].astype(jnp.float32)
            tmp[base + 3 : base + 7, :] = wgt[k, j]
            tmp[base + 7 : base + 8, :] = rate[k, j : j + 1, :]
            tmp[base + 8 : base + 9, :] = off[k, j : j + 1, :]
    for n in range(tab.shape[0] // LANES):
        tab[n * LANES : (n + 1) * LANES, :] = tmp[:, n * LANES : (n + 1) * LANES].T
    lane = lax.broadcasted_iota(jnp.int32, (8, LANES), 1)

    at = []
    first_group = 0
    moved = LANES
    for k in range(SECTIONS):
        in_beams = eighth << k
        remaining = place % (1 << (SECTIONS - k))
        in_start = remaining * in_beams
        groups = in_beams // 4
        moved -= MOVES[k]
        at.append((first_group, groups, moved))

        def plan(g, carry, k=k, in_start=in_start, groups=groups, first=first_group, moved=moved):
            rows = tab[pl.ds(pl.multiple_of(2 * in_start + 8 * g, 8), 8), :]
            for j in range(2):
                def field(q):
                    n = (k * 2 + j) * FIELDS + q
                    return jnp.broadcast_to(rows[:, n : n + 1], (8, LANES))
                to = first + j * groups + g
                local = field(0) - (in_start + 4 * g).astype(jnp.float32)
                f = field(1)
                for b in range(4):
                    coef[to, BLEND + b] = jnp.where(local == b, 1.0 - f, 0.0) + jnp.where(local == b - 1, f, 0.0)
                coef[to, FIRST] = field(2) + float(SHIFT + MOVES[k] - SHIFT - 1)
                for t in range(TAPS):
                    coef[to, WEIGHT + t] = field(3 + t)
                r = (lane - moved + col_base).astype(jnp.float32) + 0.5
                cyc = field(7)
                c0, s0 = cos_sin(cyc * (r / span) + field(8))
                c1, s1 = cos_sin(cyc * (LANES / span))
                coef[to, COS] = c0
                coef[to, SIN] = s0
                coef[to, STEP_COS] = c1
                coef[to, STEP_SIN] = s1
            return carry

        lax.fori_loop(0, groups, plan, 0)
        first_group += 2 * groups

    def merge(k, src, dst, row, rows, g, half):
        first, groups, left = at[k]
        count = blocks + 1 if k < SECTIONS - 1 else blocks
        grp = 2 * g + half
        results = []
        for j in range(2):
            to = first + j * groups + grp
            d0 = coef[to, FIRST].astype(jnp.int32)
            idx, nxt = (lane + d0) & (LANES - 1), lane < d0
            w = [coef[to, WEIGHT + t] for t in range(TAPS)]
            bl = [coef[to, BLEND + b] for b in range(4)]
            pc, ps = coef[to, COS], coef[to, SIN]
            sc, ss = coef[to, STEP_COS], coef[to, STEP_SIN]

            def angled(ch, block):
                block = block - 1 if k == 0 else block
                if block < 0 or (block + 1) * LANES > src.shape[3]:
                    return jnp.zeros((8, LANES), jnp.float32)
                tile = src[ch, rows[j], pl.ds(pl.multiple_of(8 * g, 8), 8), block * LANES : (block + 1) * LANES]
                total = None
                for b in range(4):
                    term = bl[b] * jnp.broadcast_to(tile[4 * half + b : 4 * half + b + 1, :], (8, LANES))
                    total = term if total is None else total + term
                return total

            def shifted(now, then):
                return [lane_take(jnp.where(nxt, b, a), idx) for a, b in zip(now, then)]

            def ahead_by(n, now, then):
                return pltpu.roll(jnp.where(lane < n, then, now), LANES - n, axis=1)

            def taps(now, then):
                pairs = [(a, ahead_by(1, a, b)) for a, b in zip(now, then)]
                return [w[0] * a + w[1] * b for a, b in pairs], [w[2] * a + w[3] * b for a, b in pairs]

            angles = [[angled(ch, n) for ch in range(2)] for n in range(blocks + 2)]
            shifts = [shifted(angles[n], angles[n + 1]) for n in range(blocks + 1)]
            made = [taps(shifts[n], shifts[min(n + 1, blocks)]) for n in range(blocks + 1)]
            for block in range(count):
                now, then = made[block], made[min(block + 1, blocks)]
                ranged = [now[0][ch] + ahead_by(2, now[1][ch], then[1][ch]) for ch in range(2)]
                re = ranged[0] * pc - ranged[1] * ps
                im = ranged[0] * ps + ranged[1] * pc
                if j == 0:
                    results.append((re, im))
                else:
                    results[block] = (results[block][0] + re, results[block][1] + im)
                if block < count - 1:
                    pc, ps = pc * sc - ps * ss, pc * ss + ps * sc
        for block, pair in enumerate(results):
            if k < SECTIONS - 1 and block in (0, count - 1):
                r = lane + (block * LANES - left + col_base)
                pair = [jnp.where((r >= 0) & (r < span), part, 0.0) for part in pair]
            for ch in range(2):
                at_rows = pl.ds(pl.multiple_of(8 * grp, 8), 8)
                dst[ch, row, at_rows, block * LANES : (block + 1) * LANES] = pair[ch]

    def out_copy(c):
        n = chunk * WAYS
        return pltpu.make_async_copy(
            x3.at[:, 0, pl.ds(c * n, n), pl.ds(own_at, row_len)],
            out.at[:, 0, pl.ds(c * n, n), :],
            out_sem.at[c],
        )

    def compute(c):
        buffers = (x0, x1, x2, x3)
        for k in range(SECTIONS):
            n_rows = WAYS >> (k + 1)
            pairs = (chunk << k) // 8

            def body(it, carry, k=k, n_rows=n_rows, pairs=pairs):
                row, g = it // pairs, it % pairs
                for half in range(2):
                    merge(k, buffers[k], buffers[k + 1], row, (row, row + n_rows), c * pairs + g, half)
                return carry

            lax.fori_loop(0, n_rows * pairs, body, 0)
        out_copy(c).start()

    def arrive(c):
        own_copy(c).wait()
        for x in order:
            piece(c, x, False).wait_recv()
        halo(c, True).start()

    arrive(0)
    for c in range(chunks):
        if c + 1 < chunks:
            halo(c, False).wait_recv()
            compute(c)
            arrive(c + 1)
        else:
            halo(c, False).wait_recv()
            compute(c)
    for c in range(chunks):
        for x in order:
            piece(c, x, True).wait_send()
        halo(c, True).wait_send()
        out_copy(c).wait()


def on_device(polar_image, beam_tap, beam_frac, range_shift, range_weight, phase_rate, phase_offset):
    tables = (beam_tap, beam_frac, range_shift, range_weight, phase_rate, phase_offset)
    _, sub_count, beams, row_len = polar_image.shape
    eighth = beams // WAYS
    chunk = 8
    chunks = eighth // chunk
    group_step = lax.axis_size("sub") // WAYS
    width = row_len + LANES
    positions = beam_tap.shape[2]
    hbm = pl.BlockSpec(memory_space=pl.ANY)
    n_groups = sum(2 * ((eighth << k) // 4) for k in range(SECTIONS))
    return pl.pallas_call(
        functools.partial(kernel, group_step, chunk, row_len * lax.axis_size("rng")),
        out_shape=jax.ShapeDtypeStruct(polar_image.shape, jnp.float32),
        in_specs=[hbm] * 7,
        out_specs=hbm,
        scratch_shapes=[pltpu.VMEM(a.shape, a.dtype) for a in tables]
        + [
            pltpu.VMEM((2, WAYS, eighth, width), jnp.float32),
            pltpu.VMEM((2, WAYS // 2, 2 * eighth, width + LANES), jnp.float32),
            pltpu.VMEM((2, WAYS // 4, 4 * eighth, width + LANES), jnp.float32),
            pltpu.VMEM((2, 1, beams, width), jnp.float32),
            pltpu.VMEM((LANES, positions), jnp.float32),
            pltpu.VMEM((positions, LANES), jnp.float32),
            pltpu.VMEM((n_groups, PLANES, 8, LANES), jnp.float32),
            pltpu.SemaphoreType.DMA((len(tables),)),
            pltpu.SemaphoreType.DMA((chunks, WAYS)),
            pltpu.SemaphoreType.DMA((chunks, WAYS)),
            pltpu.SemaphoreType.DMA((chunks,)),
            pltpu.SemaphoreType.DMA((chunks,)),
            pltpu.SemaphoreType.DMA((chunks,)),
            pltpu.SemaphoreType.DMA((chunks,)),
        ],
        compiler_params=pltpu.CompilerParams(
            collective_id=0, has_side_effects=True, vmem_limit_bytes=60 * 2**20
        ),
    )(polar_image, *tables)


def solution(mesh):
    placed = (P(None, "sub", None, "rng"), P(), P(), P(), P(), P(), P())
    return jax.shard_map(
        on_device,
        mesh=mesh,
        in_specs=placed,
        out_specs=P(None, "sub", None, "rng"),
        check_vma=False,
    )
```
